256 devices in a mesh: blk: 32 (over z, y_hi, core), head: 8 (over y_lo, x).
Axes of the slice: x: 4, y: 4 (y_hi: 2, y_lo: 2; y = y_hi * 2 + y_lo), z: 8, core: 2. Of those that a mesh axis runs over, the one named last changes fastest.
Arguments:
- queries: bfloat16 [32768, 4096], P(('blk', 'head')), may hold values from -7 to 7
- key_states: bfloat16 [32768, 1024], P(('blk', 'head')), may hold values from -4.5 to 4.5
- value_states: bfloat16 [32768, 1024], P(('blk', 'head')), may hold values from -6 to 6
- grad_output: bfloat16 [32768, 4096], P(('blk', 'head')), may hold values from -12 to 12
- segment_ids: int32 [32768], replicated, may hold values from 0 to 15, never falling along the last dimension, each value on 1 to 4096 neighbouring positions
Outputs:
- attn_out: bfloat16 [32768, 4096], P(('blk', 'head'))
- grad_queries: bfloat16 [32768, 4096], P(('blk', 'head'))
- grad_keys: bfloat16 [32768, 1024], P(('blk', 'head'))
- grad_values: bfloat16 [32768, 1024], P(('blk', 'head'))
The draws below stay inside these ranges and needn't reach their ends.
Inputs may be any that keep to these rules, and one draw needn't show every extreme that they name: `segment_ids`: segment numbers never fall along the sequence; equal numbers mark one trajectory.
All inputs are finite; a program needn't handle non-finite values.
Results may differ from the reference program's by a relative error of at most 0.02.
Values may be sent and summed in bfloat16 or wider, within the bound.
No kernel may reach another device: no remote copies, remote signals or barrier semaphores. Data moves between devices by JAX's collectives and lax.ppermute only.
A program may use at most 64 MiB of HBM per device.

```python
import math
import jax
import jax.numpy as jnp
import numpy as np
from jax import lax

QHEADS = 32
KVHEADS = 8
HEAD_DIM = 128
BLK_ROWS = 1024
SEQ = 32768


def draw_queries(key, part):
    key = jax.random.fold_in(key, 1)
    values = jnp.clip(jax.random.normal(key, (SEQ, QHEADS * HEAD_DIM)), -4.5, 4.5)
    return values.astype(jnp.bfloat16)


def draw_key_states(key, part):
    key = jax.random.fold_in(key, 3)
    values = jnp.clip(jax.random.normal(key, (SEQ, KVHEADS * HEAD_DIM)), -4.5, 4.5)
    return values.astype(jnp.bfloat16)


def block_levels(rng, dims, split, low, top_value):
    def one(axis_at, shards_of):
        steps = jax.random.uniform(jax.random.fold_in(jax.random.fold_in(rng, 6), axis_at), (shards_of,), jnp.float32, low / len(split), top_value / len(split))
        return jnp.repeat(jnp.exp(steps), dims[axis_at] // shards_of).reshape((-1,) + (1,) * (len(dims) - axis_at - 1))

    level = one(*split[0])
    for cut in split[1:]:
        level = level * one(*cut)
    return level


def profile(number_of, total, most, lean):
    portions = [(1 << 20) // math.isqrt(rank ** lean) + 1 for rank in range(2, number_of + 1)]
    spare, counts = total - most - (number_of - 1), [1] * (number_of - 1)
    while spare > 0:
        candidates = [i for i in range(number_of - 1) if counts[i] < most]
        pool, left = sum([portions[i] for i in candidates]), spare
        for i in candidates:
            extra = min(most - counts[i], max(1, left * portions[i] // pool), spare)
            counts[i] = counts[i] + extra
            spare = spare - extra
    return np.array([most] + counts)


def uneven(own_key, amount, total, reach, skew):
    if amount == 2:
        one = jax.random.randint(own_key, (), max(1, total - reach), min(reach, total - 1) + 1)
        return jnp.stack([one, total - one])
    sizes = jnp.asarray(profile(amount, total, reach, skew), jnp.int32)
    pairs = (amount - 1) // 2
    donor, taker = sizes[1:1 + 2 * pairs:2], sizes[2:2 + 2 * pairs:2]
    margin = jnp.minimum(donor - 1, reach - taker)
    shifted = jax.random.randint(jax.random.fold_in(own_key, 1), (pairs,), 0, 1 << 20) % (margin + 1)
    sizes = sizes.at[1:1 + 2 * pairs:2].set(donor - shifted).at[2:2 + 2 * pairs:2].set(taker + shifted)
    return sizes[jax.random.permutation(jax.random.fold_in(own_key, 2), amount)]


def gaussian(stream_key, extent, width, most, pieces=(), kind=jnp.bfloat16):
    result = jax.random.normal(stream_key, extent, jnp.float32) * width
    if len(pieces) > 0:
        result = block_levels(stream_key, extent, pieces, -0.22, 0.18) * result
    return jnp.clip(result, min=-most, max=most).astype(kind)


def setup_inputs(seed: int = 0) -> dict:
    key_of = jax.random.split(jax.random.key(seed), 6)
    return {
        "queries": draw_queries(jax.random.fold_in(key_of[5], 71), 0),
        "key_states": draw_key_states(jax.random.fold_in(key_of[5], 71), 0),
        "value_states": gaussian(key_of[2], (SEQ, KVHEADS * HEAD_DIM), 1.0, 6.0, ((0, 256),)),
        "grad_output": gaussian(key_of[3], (SEQ, QHEADS * HEAD_DIM), 2.0, 12.0, ((0, 256),)),
        "segment_ids": jnp.searchsorted(jnp.cumsum(uneven(key_of[4], SEQ // (2 * BLK_ROWS), SEQ, 4 * BLK_ROWS, 0)), jnp.arange(SEQ), side="right").astype(jnp.int32),
    }


MASKED = -1e+30

def reference(queries, key_states, value_states, grad_output, segment_ids):
    group_size = QHEADS // KVHEADS
    scaling = 1.0 / math.sqrt(HEAD_DIM)
    rows = BLK_ROWS
    block_count = SEQ // BLK_ROWS
    segment_all = segment_ids.astype(jnp.int32)
    padded_seg = jnp.concatenate([jnp.full((rows,), -1, jnp.int32), segment_all])
    key_pad = jnp.concatenate([jnp.zeros((rows, KVHEADS * HEAD_DIM), key_states.dtype), key_states], axis=0)
    value_pad = jnp.concatenate([jnp.zeros((rows, KVHEADS * HEAD_DIM), value_states.dtype), value_states], axis=0)
    row_ids = jnp.arange(rows, dtype=jnp.int32)[:, None]
    col_ids = jnp.arange(2 * rows, dtype=jnp.int32)[None, :]
    band = (col_ids > row_ids) & (col_ids <= row_ids + rows)

    def one_block(block):
        start = (block * rows).astype(jnp.int32)
        query_block = lax.dynamic_slice_in_dim(queries, start, rows).reshape(rows, KVHEADS, group_size, HEAD_DIM).transpose(1, 2, 0, 3)
        grad_block = lax.dynamic_slice_in_dim(grad_output, start, rows).reshape(rows, KVHEADS, group_size, HEAD_DIM).transpose(1, 2, 0, 3)
        key_block = lax.dynamic_slice_in_dim(key_pad, start, 2 * rows).reshape(2 * rows, KVHEADS, HEAD_DIM).transpose(1, 0, 2)
        value_block = lax.dynamic_slice_in_dim(value_pad, start, 2 * rows).reshape(2 * rows, KVHEADS, HEAD_DIM).transpose(1, 0, 2)
        query_seg = lax.dynamic_slice_in_dim(segment_all, start, rows)
        key_seg = lax.dynamic_slice_in_dim(padded_seg, start, 2 * rows)
        allowed = band & (key_seg[None, :] == query_seg[:, None])

        def one_group(inputs):
            query_group, grad_group, key_group, value_group = inputs

            def one_head(head_pair):
                query_head, grad_head = head_pair
                scores = jnp.dot(query_head, key_group.T, preferred_element_type=jnp.float32) * scaling
                scores = jnp.where(allowed, scores, MASKED)
                row_top = lax.optimization_barrier(jnp.max(scores, axis=1, keepdims=True))
                kept_terms = jnp.where(allowed, jnp.exp(scores - row_top), 0.0)
                log_total = row_top + jnp.log(lax.optimization_barrier(jnp.sum(kept_terms, axis=1, keepdims=True)))
                weights = jnp.where(allowed, jnp.exp(scores - log_total), 0.0).astype(jnp.bfloat16)
                output = jnp.dot(weights, value_group, preferred_element_type=jnp.float32).astype(jnp.bfloat16)
                row_dot = lax.optimization_barrier(jnp.sum(grad_head.astype(jnp.float32) * output.astype(jnp.float32), axis=1, keepdims=True))
                grad_weights = jnp.dot(grad_head, value_group.T, preferred_element_type=jnp.float32)
                grad_scores = (weights.astype(jnp.float32) * (grad_weights - row_dot) * scaling).astype(jnp.bfloat16)
                grad_query = jnp.dot(grad_scores, key_group, preferred_element_type=jnp.float32).astype(jnp.bfloat16)
                grad_key = jnp.dot(grad_scores.T, query_head, preferred_element_type=jnp.float32)
                grad_value = jnp.dot(weights.T, grad_head, preferred_element_type=jnp.float32)
                return (output, grad_query, grad_key, grad_value)
            results = lax.map(one_head, (query_group, grad_group))
            return (results[0], results[1], lax.optimization_barrier(jnp.sum(results[2], axis=0)), lax.optimization_barrier(jnp.sum(results[3], axis=0)))
        return lax.map(one_group, (query_block, grad_block, key_block, value_block))
    outputs, grad_query_parts, key_parts, value_parts = lax.map(one_block, jnp.arange(block_count, dtype=jnp.int32))
    attn_out = outputs.transpose(0, 3, 1, 2, 4).reshape(SEQ, QHEADS * HEAD_DIM)
    grad_queries = grad_query_parts.transpose(0, 3, 1, 2, 4).reshape(SEQ, QHEADS * HEAD_DIM)

    def combine(parts):
        own = parts[:, :, rows:]
        earlier = parts[:, :, :rows]
        from_next = jnp.concatenate([earlier[1:], jnp.zeros_like(earlier[:1])], axis=0)
        total = own + from_next
        return total.transpose(0, 2, 1, 3).reshape(SEQ, KVHEADS * HEAD_DIM).astype(jnp.bfloat16)
    return (attn_out, grad_queries, combine(key_parts), combine(value_parts))
```

```python
import functools
import math

import jax
import jax.numpy as jnp
from jax import lax
from jax.experimental import pallas as pl
from jax.experimental.pallas import tpu as pltpu
from jax.sharding import PartitionSpec as P

HEAD_DIM = 128
WINDOW = 1024
RING = 4
TOK = 128
ROWS = RING * TOK
GROUP = 4
KV = 2
HALF = GROUP * HEAD_DIM
EXT = ROWS + WINDOW
SCALE = 1.0 / math.sqrt(HEAD_DIM)
LOG2E = math.log2(math.e)
BIG = 16384.0
BF = jnp.bfloat16
F32 = jnp.float32
NT = (((1,), (1,)), ((), ()))
TN = (((0,), (0,)), ((), ()))


def attend(g, pos_ref, qseg_ref, kseg_ref, *refs):
    qin, (kvo, kv1, kv2) = refs[:4], refs[4:7]
    outs, (dko, dk1, dk2) = refs[7:11], refs[11:14]
    kx, vx, acck, accv, qs, dos, res, qn, gn, dots, invs, s_scr, p_scr, d_scr = refs[14:]

    for src, base in ((kv2, 0), (kv1, ROWS), (kvo, 2 * ROWS)):
        for d in range(RING):
            row = pl.ds(pl.multiple_of(base + TOK * pos_ref[d], TOK), TOK)
            kx[row, :HEAD_DIM] = src[TOK * d : TOK * (d + 1), HEAD_DIM * g : HEAD_DIM * (g + 1)]
            vx[row, :HEAD_DIM] = src[
                TOK * d : TOK * (d + 1), HEAD_DIM * (KV + g) : HEAD_DIM * (KV + g + 1)
            ]
    kx[:, HEAD_DIM:] = kseg_ref[...]
    vx[:, HEAD_DIM:] = jnp.ones((EXT, HEAD_DIM), BF)
    acck[...] = jnp.zeros_like(acck)
    accv[...] = jnp.zeros_like(accv)
    for d in range(RING):
        seg = qseg_ref[pl.ds(pl.multiple_of(TOK * pos_ref[d], TOK), TOK)]
        for j in range(GROUP):
            sl = slice(TOK * j, TOK * (j + 1))
            qs[d, sl, :HEAD_DIM] = qin[d][:, HEAD_DIM * j : HEAD_DIM * (j + 1)]
            qs[d, sl, HEAD_DIM:] = seg
            dos[d, sl] = qin[d][:, HALF + HEAD_DIM * j : HALF + HEAD_DIM * (j + 1)]

    row_id = lax.broadcasted_iota(jnp.int32, (TOK, TOK), 0)
    col_id = lax.broadcasted_iota(jnp.int32, (TOK, TOK), 1)
    lower = col_id <= row_id

    def step(d, carry):
        start = pl.multiple_of(TOK * pos_ref[d], TOK)
        span = pl.ds(start, WINDOW + TOK)
        s_scr[...] = lax.dot_general(qs[d], kx[span], NT, preferred_element_type=F32)
        for j in range(GROUP):
            sl = slice(TOK * j, TOK * (j + 1))
            edge = jnp.where(lower, s_scr[sl, WINDOW:], s_scr[sl, :TOK])
            body = s_scr[sl, TOK:WINDOW]
            top = jnp.maximum(
                jnp.max(edge, axis=1, keepdims=True), jnp.max(body, axis=1, keepdims=True)
            )
            edge = jnp.exp2((edge - top) * (SCALE * LOG2E))
            p_scr[sl, :TOK] = jnp.where(lower, 0.0, edge).astype(BF)
            p_scr[sl, WINDOW:] = jnp.where(lower, edge, 0.0).astype(BF)
            p_scr[sl, TOK:WINDOW] = jnp.exp2((body - top) * (SCALE * LOG2E)).astype(BF)
        for j in range(0, ROWS, 256):
            sl = slice(j, j + 256)
            out = jnp.dot(p_scr[sl], vx[span], preferred_element_type=F32)
            inv = 1.0 / out[:, HEAD_DIM:]
            attn = (out[:, :HEAD_DIM] * inv).astype(BF)
            res[d, sl, :HEAD_DIM] = attn
            grad = dos[d, sl].astype(F32)
            dots[sl] = jnp.sum(grad * attn.astype(F32), axis=1, keepdims=True)
            invs[sl] = inv * SCALE
            qn[sl] = (qs[d, sl, :HEAD_DIM].astype(F32) * (inv * SCALE)).astype(BF)
            gn[sl] = (grad * inv).astype(BF)
        d_scr[...] = (
            (lax.dot_general(dos[d], vx[span, :HEAD_DIM], NT, preferred_element_type=F32) - dots[...])
            * p_scr[...].astype(F32)
        ).astype(BF)
        for j in range(0, ROWS, 256):
            sl = slice(j, j + 256)
            dq = jnp.dot(d_scr[sl], kx[span, :HEAD_DIM], preferred_element_type=F32)
            res[d, sl, HEAD_DIM:] = (dq * invs[sl]).astype(BF)
        acck[:, span] += lax.dot_general(qn[...], d_scr[...], TN, preferred_element_type=F32)
        accv[:, span] += lax.dot_general(gn[...], p_scr[...], TN, preferred_element_type=F32)
        return carry

    lax.fori_loop(0, RING, step, 0)

    for d in range(RING):
        for j in range(GROUP):
            sl = slice(TOK * j, TOK * (j + 1))
            outs[d][:, HEAD_DIM * j : HEAD_DIM * (j + 1)] = res[d, sl, :HEAD_DIM]
            outs[d][:, HALF + HEAD_DIM * j : HALF + HEAD_DIM * (j + 1)] = res[d, sl, HEAD_DIM:]
    for dst, base in ((dk2, 0), (dk1, ROWS), (dko, 2 * ROWS)):
        for d in range(RING):
            row = pl.ds(pl.multiple_of(base + TOK * pos_ref[d], TOK), TOK)
            sl = slice(TOK * d, TOK * (d + 1))
            dst[sl, :HEAD_DIM] = acck[:, row].T.astype(dst.dtype)
            dst[sl, HEAD_DIM:] = accv[:, row].T.astype(dst.dtype)


def call(body, name, shapes, args, scratch=(), flops=0, limit=60):
    vm = pl.BlockSpec(memory_space=pltpu.VMEM)
    sm = pl.BlockSpec(memory_space=pltpu.SMEM)
    return list(
        pl.pallas_call(
            body,
            out_shape=[jax.ShapeDtypeStruct(shape, dtype) for shape, dtype in shapes],
            in_specs=[sm if arg.ndim == 1 else vm for arg in args],
            out_specs=[vm] * len(shapes),
            scratch_shapes=[pltpu.VMEM(shape, dtype) for shape, dtype in scratch],
            compiler_params=pltpu.CompilerParams(vmem_limit_bytes=limit * 1024 * 1024),
            cost_estimate=pl.CostEstimate(
                flops=flops, bytes_accessed=4 * 1024 * 1024, transcendentals=0
            ),
            name=name,
        )(*args)
    )


def attend_call(g, pos, qseg, kseg, qin, kvs):
    return call(
        functools.partial(attend, g),
        "attend",
        [((TOK, 2 * HALF), BF)] * RING
        + [((ROWS, 2 * HEAD_DIM), F32)]
        + [((ROWS, 2 * HEAD_DIM), BF)] * 2,
        (pos, qseg, kseg, *qin, *kvs),
        [
            ((EXT, 2 * HEAD_DIM), BF),
            ((EXT, 2 * HEAD_DIM), BF),
            ((HEAD_DIM, EXT), F32),
            ((HEAD_DIM, EXT), F32),
            ((RING, ROWS, 2 * HEAD_DIM), BF),
            ((RING, ROWS, HEAD_DIM), BF),
            ((RING, ROWS, 2 * HEAD_DIM), BF),
            ((ROWS, HEAD_DIM), BF),
            ((ROWS, HEAD_DIM), BF),
            ((ROWS, 1), F32),
            ((ROWS, HEAD_DIM), F32),
            ((ROWS, WINDOW + TOK), F32),
            ((ROWS, WINDOW + TOK), BF),
            ((ROWS, WINDOW + TOK), BF),
        ],
        flops=6 * 2 * 4 * ROWS * 1152 * 256,
        limit=60,
    )


def ring_slice(here_ref, steps, width):
    at = lax.rem(here_ref[0] + (steps + RING), RING)
    return pl.ds(pl.multiple_of(at * width, width), width)


def pack_kv(here_ref, k_ref, v_ref, *outs):
    width = KV * HEAD_DIM
    for d in range(RING):
        cols = ring_slice(here_ref, d, width)
        outs[d][:, :width] = k_ref[:, cols]
        outs[d][:, width:] = v_ref[:, cols]


def pack_q(here_ref, q_ref, d_ref, *outs):
    for d in range(RING):
        cols = ring_slice(here_ref, d, KV * HALF)
        for ref, base in ((q_ref, 0), (d_ref, HALF)):
            value = ref[:, cols]
            for g in range(KV):
                outs[g * RING + d][:, base : base + HALF] = value[:, g * HALF : (g + 1) * HALF]


def add_kv(own0, one0, two0, own1, one1, two1, *outs):
    for g, (own, one, two) in enumerate(((own0, one0, two0), (own1, one1, two1))):
        for d in range(RING):
            rows = slice(TOK * d, TOK * (d + 1))
            total = own[rows] + one[rows].astype(F32) + two[rows].astype(F32)
            outs[d][:, 2 * HEAD_DIM * g : 2 * HEAD_DIM * (g + 1)] = total.astype(BF)


def assemble(here_ref, *refs):
    parts, kvs, (attn, gq, gk, gv) = refs[: 2 * RING], refs[2 * RING : 3 * RING], refs[3 * RING :]
    for d in range(RING):
        wide = ring_slice(here_ref, d, KV * HALF)
        thin = ring_slice(here_ref, d, KV * HEAD_DIM)
        for ref, base in ((attn, 0), (gq, HALF)):
            ref[:, wide] = jnp.concatenate(
                [parts[g * RING + d][:, base : base + HALF] for g in range(KV)], axis=1
            )
        for ref, base in ((gk, 0), (gv, HEAD_DIM)):
            ref[:, thin] = jnp.concatenate(
                [
                    kvs[d][:, base + 2 * HEAD_DIM * g : base + 2 * HEAD_DIM * g + HEAD_DIM]
                    for g in range(KV)
                ],
                axis=1,
            )


def shards(queries, key_states, value_states, grad_output, segment_ids):
    heads = lax.axis_size("head")
    halves = lax.axis_size("blk") * heads // RING
    head = lax.axis_index("head")
    index = head % RING
    here = jnp.full((1,), index, jnp.int32)
    half = (lax.axis_index("blk") * heads + head) // RING

    def along_ring(value, steps):
        pairs = [(i, i // RING * RING + (i + steps) % RING) for i in range(heads)]
        return lax.ppermute(value, "head", pairs)

    def along_halves(value, steps):
        pairs = [
            (i * RING + x, (i + steps) * RING + x)
            for i in range(max(0, -steps), min(halves, halves - steps))
            for x in range(RING)
        ]
        return lax.ppermute(value, ("blk", "head"), pairs)

    def around(parts, sign):
        return parts[:1] + [along_ring(parts[d], sign * d) for d in range(1, RING)]

    thin_part, wide_part = ((TOK, 2 * KV * HEAD_DIM), BF), ((TOK, 2 * HALF), BF)
    kv = call(pack_kv, "pack_kv", [thin_part] * RING, (here, key_states, value_states))
    packed = call(pack_q, "pack_q", [wide_part] * (KV * RING), (here, queries, grad_output))
    kv_own = jnp.concatenate(around(kv, 1), axis=0)
    kv_own, packed = lax.optimization_barrier((kv_own, packed))
    kvs = (kv_own, along_halves(kv_own, 1), along_halves(kv_own, 2))
    first, second = around(packed[:RING], 1), packed[RING:]
    first, second = lax.optimization_barrier((first, second))
    q_parts = (first, around(second, 1))

    padded = jnp.concatenate([jnp.full((WINDOW,), HEAD_DIM - 1, jnp.int32), segment_ids])
    key_seg = lax.dynamic_slice_in_dim(padded, half * ROWS, EXT)
    lanes = jnp.arange(HEAD_DIM, dtype=jnp.int32)[None, :]
    kseg = (key_seg[:, None] == lanes).astype(BF)
    qseg = jnp.where(key_seg[WINDOW:, None] == lanes, 0.0, -BIG).astype(BF)
    steps = jnp.arange(RING, dtype=jnp.int32)
    pos = (index - steps) % RING

    wide, thin = [], []
    for g in range(KV):
        res = attend_call(g, pos, qseg, kseg, q_parts[g], kvs)
        if g > 0:
            res, wide, thin = lax.optimization_barrier((res, wide, thin))
        thin += [res[4], along_halves(res[5], -1), along_halves(res[6], -2)]
        wide += around(res[:RING], -1)
    grads = around(call(add_kv, "add_kv", [thin_part] * RING, thin), -1)
    width = RING * KV * HALF
    return tuple(
        call(
            assemble,
            "assemble",
            [((TOK, width), BF)] * 2 + [((TOK, width // GROUP), BF)] * 2,
            (here, *wide, *grads),
        )
    )


def solution(mesh):
    placed = P(("blk", "head"), None)
    return jax.shard_map(
        shards,
        mesh=mesh,
        in_specs=(placed, placed, placed, placed, P()),
        out_specs=(placed, placed, placed, placed),
        check_vma=False,
    )
```

```python
import functools
import math

import jax
import jax.numpy as jnp
from jax import lax
from jax.experimental import pallas as pl
from jax.experimental.pallas import tpu as pltpu
from jax.sharding import PartitionSpec as P

HEAD_DIM = 128
WINDOW = 1024
RING = 4
TOK = 128
ROWS = RING * TOK
GROUP = 4
KV = 2
HALF = GROUP * HEAD_DIM
EXT = ROWS + WINDOW
SCALE = 1.0 / math.sqrt(HEAD_DIM)
LOG2E = math.log2(math.e)
BIG = 16384.0
BF = jnp.bfloat16
F32 = jnp.float32
NT = (((1,), (1,)), ((), ()))
TN = (((0,), (0,)), ((), ()))


def attend(g, n_earlier, pos_ref, qseg_ref, kseg_ref, *refs):
    qin, (kvo, kv1, kv2) = refs[:4], refs[4:7]
    earlier, refs = refs[7 : 7 + n_earlier], refs[7 + n_earlier :]
    outs, (dko, dk1, dk2) = refs[:4], refs[4:7]
    kx, vx, acck, accv, qs, dos, res, qn, gn, dots, invs, s_scr, p_scr, d_scr = refs[7:]

    for src, base in ((kv2, 0), (kv1, ROWS), (kvo, 2 * ROWS)):
        for d in range(RING):
            row = pl.ds(pl.multiple_of(base + TOK * pos_ref[d], TOK), TOK)
            kx[row, :HEAD_DIM] = src[TOK * d : TOK * (d + 1), :HEAD_DIM]
            vx[row, :HEAD_DIM] = src[TOK * d : TOK * (d + 1), HEAD_DIM:]
    kx[:, HEAD_DIM:] = kseg_ref[...]
    vx[:, HEAD_DIM:] = jnp.ones((EXT, HEAD_DIM), BF)
    acck[...] = jnp.zeros_like(acck)
    accv[...] = jnp.zeros_like(accv)
    for d in range(RING):
        seg = qseg_ref[pl.ds(pl.multiple_of(TOK * pos_ref[d], TOK), TOK)]
        for j in range(GROUP):
            sl = slice(TOK * j, TOK * (j + 1))
            qs[d, sl, :HEAD_DIM] = qin[d][:, HEAD_DIM * j : HEAD_DIM * (j + 1)]
            qs[d, sl, HEAD_DIM:] = seg
            dos[d, sl] = qin[d][:, HALF + HEAD_DIM * j : HALF + HEAD_DIM * (j + 1)]

    row_id = lax.broadcasted_iota(jnp.int32, (TOK, TOK), 0)
    col_id = lax.broadcasted_iota(jnp.int32, (TOK, TOK), 1)
    lower = col_id <= row_id

    def step(d, carry):
        start = pl.multiple_of(TOK * pos_ref[d], TOK)
        span = pl.ds(start, WINDOW + TOK)
        s_scr[...] = lax.dot_general(qs[d], kx[span], NT, preferred_element_type=F32)
        for j in range(GROUP):
            sl = slice(TOK * j, TOK * (j + 1))
            edge = jnp.where(lower, s_scr[sl, WINDOW:], s_scr[sl, :TOK])
            body = s_scr[sl, TOK:WINDOW]
            top = jnp.maximum(
                jnp.max(edge, axis=1, keepdims=True), jnp.max(body, axis=1, keepdims=True)
            )
            edge = jnp.exp2((edge - top) * (SCALE * LOG2E))
            p_scr[sl, :TOK] = jnp.where(lower, 0.0, edge).astype(BF)
            p_scr[sl, WINDOW:] = jnp.where(lower, edge, 0.0).astype(BF)
            p_scr[sl, TOK:WINDOW] = jnp.exp2((body - top) * (SCALE * LOG2E)).astype(BF)
        for j in range(0, ROWS, 256):
            sl = slice(j, j + 256)
            out = jnp.dot(p_scr[sl], vx[span], preferred_element_type=F32)
            inv = 1.0 / out[:, HEAD_DIM:]
            attn = (out[:, :HEAD_DIM] * inv).astype(BF)
            res[d, sl, :HEAD_DIM] = attn
            grad = dos[d, sl].astype(F32)
            dots[sl] = jnp.sum(grad * attn.astype(F32), axis=1, keepdims=True)
            invs[sl] = inv * SCALE
            qn[sl] = (qs[d, sl, :HEAD_DIM].astype(F32) * (inv * SCALE)).astype(BF)
            gn[sl] = (grad * inv).astype(BF)
        d_scr[...] = (
            (lax.dot_general(dos[d], vx[span, :HEAD_DIM], NT, preferred_element_type=F32) - dots[...])
            * p_scr[...].astype(F32)
        ).astype(BF)
        for j in range(0, ROWS, 256):
            sl = slice(j, j + 256)
            dq = jnp.dot(d_scr[sl], kx[span, :HEAD_DIM], preferred_element_type=F32)
            res[d, sl, HEAD_DIM:] = (dq * invs[sl]).astype(BF)
        acck[:, span] += lax.dot_general(qn[...], d_scr[...], TN, preferred_element_type=F32)
        accv[:, span] += lax.dot_general(gn[...], p_scr[...], TN, preferred_element_type=F32)
        return carry

    lax.fori_loop(0, RING, step, 0)

    for d in range(RING):
        for j in range(GROUP):
            sl = slice(TOK * j, TOK * (j + 1))
            outs[d][:, HEAD_DIM * j : HEAD_DIM * (j + 1)] = res[d, sl, :HEAD_DIM]
            outs[d][:, HALF + HEAD_DIM * j : HALF + HEAD_DIM * (j + 1)] = res[d, sl, HEAD_DIM:]
    for dst, src in zip((dk1, dk2), earlier):
        dst[:, : src.shape[1]] = src[...]
    for dst, base in ((dk2, 0), (dk1, ROWS), (dko, 2 * ROWS)):
        at = dst.shape[1] - 2 * HEAD_DIM
        for d in range(RING):
            row = pl.ds(pl.multiple_of(base + TOK * pos_ref[d], TOK), TOK)
            sl = slice(TOK * d, TOK * (d + 1))
            dst[sl, at : at + HEAD_DIM] = acck[:, row].T.astype(dst.dtype)
            dst[sl, at + HEAD_DIM :] = accv[:, row].T.astype(dst.dtype)


def call(body, name, shapes, args, scratch=(), flops=0, limit=60, space=pltpu.VMEM, aliases=None):
    at = pl.BlockSpec(memory_space=space)
    vm = pl.BlockSpec(memory_space=pltpu.VMEM)
    sm = pl.BlockSpec(memory_space=pltpu.SMEM)
    return list(
        pl.pallas_call(
            body,
            out_shape=[jax.ShapeDtypeStruct(shape, dtype) for shape, dtype in shapes],
            in_specs=[
                sm if arg.ndim == 1 else at if i in (aliases or {}) else vm
                for i, arg in enumerate(args)
            ],
            out_specs=[at] * len(shapes),
            scratch_shapes=list(scratch),
            input_output_aliases=aliases or {},
            compiler_params=pltpu.CompilerParams(vmem_limit_bytes=limit * 1024 * 1024),
            cost_estimate=pl.CostEstimate(
                flops=flops, bytes_accessed=4 * 1024 * 1024, transcendentals=0
            ),
            name=name,
        )(*args)
    )


def attend_call(g, pos, qseg, kseg, qin, kvs, earlier=()):
    width = 2 * HEAD_DIM * (g + 1)
    scratch = [
        ((EXT, 2 * HEAD_DIM), BF),
        ((EXT, 2 * HEAD_DIM), BF),
        ((HEAD_DIM, EXT), F32),
        ((HEAD_DIM, EXT), F32),
        ((RING, ROWS, 2 * HEAD_DIM), BF),
        ((RING, ROWS, HEAD_DIM), BF),
        ((RING, ROWS, 2 * HEAD_DIM), BF),
        ((ROWS, HEAD_DIM), BF),
        ((ROWS, HEAD_DIM), BF),
        ((ROWS, 1), F32),
        ((ROWS, HEAD_DIM), F32),
        ((ROWS, WINDOW + TOK), F32),
        ((ROWS, WINDOW + TOK), BF),
        ((ROWS, WINDOW + TOK), BF),
    ]
    return call(
        functools.partial(attend, g, len(earlier)),
        "attend",
        [((TOK, 2 * HALF), BF)] * RING
        + [((ROWS, 2 * HEAD_DIM), F32)]
        + [((ROWS, width), BF)] * 2,
        (pos, qseg, kseg, *qin, *kvs, *earlier),
        [pltpu.VMEM(shape, dtype) for shape, dtype in scratch],
        flops=6 * 2 * 4 * ROWS * 1152 * 256,
        limit=40,
    )


def ring_slice(here_ref, steps, width):
    at = lax.rem(here_ref[0] + (steps + RING), RING)
    return pl.ds(pl.multiple_of(at * width, width), width)


def pack_kv(here_ref, k_ref, v_ref, *outs):
    for d in range(RING):
        cols = ring_slice(here_ref, d, KV * HEAD_DIM)
        for ref, base in ((k_ref, 0), (v_ref, HEAD_DIM)):
            value = ref[:, cols]
            for g in range(KV):
                at = 2 * g * HEAD_DIM + base
                outs[d][:, at : at + HEAD_DIM] = value[:, g * HEAD_DIM : (g + 1) * HEAD_DIM]


def pack_q(here_ref, q_ref, d_ref, *outs):
    for d in range(RING):
        cols = ring_slice(here_ref, d, KV * HALF)
        for ref, base in ((q_ref, 0), (d_ref, HALF)):
            value = ref[:, cols]
            for g in range(KV):
                outs[g * RING + d][:, base : base + HALF] = value[:, g * HALF : (g + 1) * HALF]


def add_kv(own0, own1, one, two, *outs):
    for g, own in enumerate((own0, own1)):
        cols = slice(2 * HEAD_DIM * g, 2 * HEAD_DIM * (g + 1))
        for d in range(RING):
            rows = slice(TOK * d, TOK * (d + 1))
            total = own[rows] + one[rows, cols].astype(F32) + two[rows, cols].astype(F32)
            outs[d][:, cols] = total.astype(BF)


def columns(index, width):
    return pl.ds(pl.multiple_of(index * width, width), width)


def place_wide(g, here_ref, parts, attn, gq, sem):
    copies = []
    for d in range(RING):
        cols = columns(lax.rem(here_ref[0] + d, RING) * KV + g, HALF)
        for dst, base in ((attn, 0), (gq, HALF)):
            src = parts[d].at[:, base : base + HALF]
            copies.append(pltpu.make_async_copy(src, dst.at[:, cols], sem.at[len(copies)]))
    return copies


def assemble_first(here_ref, *refs):
    parts, (attn, gq, sem) = refs[:RING], refs[RING:]
    copies = place_wide(0, here_ref, parts, attn, gq, sem)
    for copy in copies:
        copy.start()
    for copy in copies:
        copy.wait()


def assemble(here_ref, *refs):
    parts, kvs = refs[2 : 2 + RING], refs[2 + RING : 2 + 2 * RING]
    attn, gq, gk, gv, sem = refs[2 + 2 * RING :]
    copies = place_wide(1, here_ref, parts, attn, gq, sem)
    for d in range(RING):
        for g in range(KV):
            cols = columns(lax.rem(here_ref[0] + d, RING) * KV + g, HEAD_DIM)
            for dst, base in ((gk, 2 * g * HEAD_DIM), (gv, (2 * g + 1) * HEAD_DIM)):
                src = kvs[d].at[:, base : base + HEAD_DIM]
                copies.append(pltpu.make_async_copy(src, dst.at[:, cols], sem.at[len(copies)]))
    for copy in copies:
        copy.start()
    for copy in copies:
        copy.wait()


def shards(queries, key_states, value_states, grad_output, segment_ids):
    heads = lax.axis_size("head")
    halves = lax.axis_size("blk") * heads // RING
    head = lax.axis_index("head")
    index = head % RING
    here = jnp.full((1,), index, jnp.int32)
    half = (lax.axis_index("blk") * heads + head) // RING

    def along_ring(value, steps):
        pairs = [(i, i // RING * RING + (i + steps) % RING) for i in range(heads)]
        return lax.ppermute(value, "head", pairs)

    def along_halves(value, steps):
        pairs = [
            (i * RING + x, (i + steps) * RING + x)
            for i in range(max(0, -steps), min(halves, halves - steps))
            for x in range(RING)
        ]
        return lax.ppermute(value, ("blk", "head"), pairs)

    def around(parts, sign):
        return parts[:1] + [along_ring(parts[d], sign * d) for d in range(1, RING)]

    thin_part, wide_part = ((TOK, 2 * KV * HEAD_DIM), BF), ((TOK, 2 * HALF), BF)
    kv = call(pack_kv, "pack_kv", [thin_part] * RING, (here, key_states, value_states))
    packed = call(pack_q, "pack_q", [wide_part] * (KV * RING), (here, queries, grad_output))
    kv = around(kv, 1)
    first, second = around(packed[:RING], 1), packed[RING:]
    kvs = []
    for g in range(KV):
        cols = slice(2 * HEAD_DIM * g, 2 * HEAD_DIM * (g + 1))
        own = jnp.concatenate([part[:, cols] for part in kv], axis=0)
        kvs.append((own, along_halves(own, 1), along_halves(own, 2)))
    second, _ = lax.optimization_barrier((second, kvs[0][0]))
    q_parts = (first, around(second, 1))

    padded = jnp.concatenate([jnp.full((WINDOW,), HEAD_DIM - 1, jnp.int32), segment_ids])
    key_seg = lax.dynamic_slice_in_dim(padded, half * ROWS, EXT)
    lanes = jnp.arange(HEAD_DIM, dtype=jnp.int32)[None, :]
    kseg = (key_seg[:, None] == lanes).astype(BF)
    qseg = jnp.where(key_seg[WINDOW:, None] == lanes, 0.0, -BIG).astype(BF)
    steps = jnp.arange(RING, dtype=jnp.int32)
    pos = (index - steps) % RING

    width = RING * KV * HALF
    wide_out, thin_out = ((TOK, width), BF), ((TOK, width // GROUP), BF)
    res0 = attend_call(0, pos, qseg, kseg, q_parts[0], kvs[0])
    wide0 = around(res0[:RING], -1)
    res1 = attend_call(1, pos, qseg, kseg, q_parts[1], kvs[1], res0[5:])
    res1, wide0 = lax.optimization_barrier((res1, wide0))
    one, two = along_halves(res1[5], -1), along_halves(res1[6], -2)
    wide1 = around(res1[:RING], -1)
    placed = call(
        assemble_first,
        "assemble_first",
        [wide_out] * 2,
        (here, *wide0),
        [pltpu.SemaphoreType.DMA((2 * RING,))],
        limit=16,
        space=pl.ANY,
    )
    grads = call(add_kv, "add_kv", [thin_part] * RING, (res0[4], res1[4], one, two), limit=16)
    grads = around(grads, -1)
    return tuple(
        call(
            assemble,
            "assemble",
            [wide_out] * 2 + [thin_out] * 2,
            (here, *placed, *wide1, *grads),
            [pltpu.SemaphoreType.DMA((6 * RING,))],
            limit=16,
            space=pl.ANY,
            aliases={1: 0, 2: 1},
        )
    )


def solution(mesh):
    placed = P(("blk", "head"), None)
    return jax.shard_map(
        shards,
        mesh=mesh,
        in_specs=(placed, placed, placed, placed, P()),
        out_specs=(placed, placed, placed, placed),
        check_vma=False,
    )
```

```python
import functools
import math

import jax
import jax.numpy as jnp
from jax import lax
from jax.experimental import pallas as pl
from jax.experimental.pallas import tpu as pltpu
from jax.sharding import PartitionSpec as P

HEAD_DIM = 128
WINDOW = 1024
RING = 4
TOK = 128
ROWS = RING * TOK
GROUP = 4
KV = 2
HALF = GROUP * HEAD_DIM
EXT = ROWS + WINDOW
SCALE = 1.0 / math.sqrt(HEAD_DIM)
LOG2E = math.log2(math.e)
BIG = 16384.0
BF = jnp.bfloat16
F32 = jnp.float32
NT = (((1,), (1,)), ((), ()))
TN = (((0,), (0,)), ((), ()))


def attend(g, n_earlier, pos_ref, qseg_ref, kseg_ref, *refs):
    qin, (kvo, kv1, kv2) = refs[:4], refs[4:7]
    earlier, refs = refs[7 : 7 + n_earlier], refs[7 + n_earlier :]
    outs, (dko, dk1, dk2) = refs[:4], refs[4:7]
    kx, vx, acck, accv, qs, dos, qn, gn, dots, invs, s_scr, p_scr, d_scr = refs[7:]

    for src, base in ((kv2, 0), (kv1, ROWS), (kvo, 2 * ROWS)):
        for d in range(RING):
            row = pl.ds(pl.multiple_of(base + TOK * pos_ref[d], TOK), TOK)
            kx[row, :HEAD_DIM] = src[TOK * d : TOK * (d + 1), :HEAD_DIM]
            vx[row, :HEAD_DIM] = src[TOK * d : TOK * (d + 1), HEAD_DIM:]
    kx[:, HEAD_DIM:] = kseg_ref[...]
    vx[:, HEAD_DIM:] = jnp.ones((EXT, HEAD_DIM), BF)
    acck[...] = jnp.zeros_like(acck)
    accv[...] = jnp.zeros_like(accv)
    for d in range(RING):
        seg = qseg_ref[pl.ds(pl.multiple_of(TOK * pos_ref[d], TOK), TOK)]
        for j in range(GROUP):
            sl = slice(TOK * j, TOK * (j + 1))
            qs[d, sl, :HEAD_DIM] = qin[d][:, HEAD_DIM * j : HEAD_DIM * (j + 1)]
            qs[d, sl, HEAD_DIM:] = seg
            dos[d, sl] = qin[d][:, HALF + HEAD_DIM * j : HALF + HEAD_DIM * (j + 1)]

    row_id = lax.broadcasted_iota(jnp.int32, (TOK, TOK), 0)
    col_id = lax.broadcasted_iota(jnp.int32, (TOK, TOK), 1)
    lower = col_id <= row_id

    def put(ref, row, base, value):
        for i in range(value.shape[0] // TOK):
            at = base + (row // TOK + i) * HEAD_DIM
            ref[:, at : at + HEAD_DIM] = value[TOK * i : TOK * (i + 1)]

    def step(d, carry):
        start = pl.multiple_of(TOK * pos_ref[d], TOK)
        span = pl.ds(start, WINDOW + TOK)
        s_scr[...] = lax.dot_general(qs[d], kx[span], NT, preferred_element_type=F32)
        for j in range(GROUP):
            sl = slice(TOK * j, TOK * (j + 1))
            edge = jnp.where(lower, s_scr[sl, WINDOW:], s_scr[sl, :TOK])
            body = s_scr[sl, TOK:WINDOW]
            top = jnp.maximum(
                jnp.max(edge, axis=1, keepdims=True), jnp.max(body, axis=1, keepdims=True)
            )
            edge = jnp.exp2((edge - top) * (SCALE * LOG2E))
            p_scr[sl, :TOK] = jnp.where(lower, 0.0, edge).astype(BF)
            p_scr[sl, WINDOW:] = jnp.where(lower, edge, 0.0).astype(BF)
            p_scr[sl, TOK:WINDOW] = jnp.exp2((body - top) * (SCALE * LOG2E)).astype(BF)
        for j in range(0, ROWS, 256):
            sl = slice(j, j + 256)
            out = jnp.dot(p_scr[sl], vx[span], preferred_element_type=F32)
            inv = 1.0 / out[:, HEAD_DIM:]
            attn = (out[:, :HEAD_DIM] * inv).astype(BF)
            put(outs[d], j, 0, attn)
            grad = dos[d, sl].astype(F32)
            dots[sl] = jnp.sum(grad * attn.astype(F32), axis=1, keepdims=True)
            invs[sl] = inv * SCALE
            qn[sl] = (qs[d, sl, :HEAD_DIM].astype(F32) * (inv * SCALE)).astype(BF)
            gn[sl] = (grad * inv).astype(BF)
        d_scr[...] = (
            (lax.dot_general(dos[d], vx[span, :HEAD_DIM], NT, preferred_element_type=F32) - dots[...])
            * p_scr[...].astype(F32)
        ).astype(BF)
        for j in range(0, ROWS, 256):
            sl = slice(j, j + 256)
            dq = jnp.dot(d_scr[sl], kx[span, :HEAD_DIM], preferred_element_type=F32)
            put(outs[d], j, HALF, (dq * invs[sl]).astype(BF))
        acck[:, span] += lax.dot_general(qn[...], d_scr[...], TN, preferred_element_type=F32)
        accv[:, span] += lax.dot_general(gn[...], p_scr[...], TN, preferred_element_type=F32)
        return carry

    for d in range(RING):
        step(d, 0)

    for dst, src in zip((dk1, dk2), earlier):
        dst[:, : src.shape[1]] = src[...]
    for dst, base in ((dk2, 0), (dk1, ROWS), (dko, 2 * ROWS)):
        at = dst.shape[1] - 2 * HEAD_DIM
        for d in range(RING):
            row = pl.ds(pl.multiple_of(base + TOK * pos_ref[d], TOK), TOK)
            sl = slice(TOK * d, TOK * (d + 1))
            dst[sl, at : at + HEAD_DIM] = acck[:, row].T.astype(dst.dtype)
            dst[sl, at + HEAD_DIM :] = accv[:, row].T.astype(dst.dtype)


def call(
    body,
    name,
    shapes,
    args,
    scratch=(),
    flops=0,
    limit=60,
    space=pltpu.VMEM,
    aliases=None,
    raw=False,
):
    at = pl.BlockSpec(memory_space=space)
    vm = pl.BlockSpec(memory_space=pltpu.VMEM)
    hbm = pl.BlockSpec(memory_space=pl.ANY)
    sm = pl.BlockSpec(memory_space=pltpu.SMEM)
    return list(
        pl.pallas_call(
            body,
            out_shape=[jax.ShapeDtypeStruct(shape, dtype) for shape, dtype in shapes],
            in_specs=[
                sm if arg.ndim == 1 else hbm if raw or i in (aliases or {}) else vm
                for i, arg in enumerate(args)
            ],
            out_specs=[at] * len(shapes),
            scratch_shapes=list(scratch),
            input_output_aliases=aliases or {},
            compiler_params=pltpu.CompilerParams(vmem_limit_bytes=limit * 1024 * 1024),
            cost_estimate=pl.CostEstimate(
                flops=flops, bytes_accessed=4 * 1024 * 1024, transcendentals=0
            ),
            name=name,
        )(*args)
    )


def attend_call(g, pos, qseg, kseg, qin, kvs, earlier=()):
    width = 2 * HEAD_DIM * (g + 1)
    scratch = [
        ((EXT, 2 * HEAD_DIM), BF),
        ((EXT, 2 * HEAD_DIM), BF),
        ((HEAD_DIM, EXT), F32),
        ((HEAD_DIM, EXT), F32),
        ((RING, ROWS, 2 * HEAD_DIM), BF),
        ((RING, ROWS, HEAD_DIM), BF),
        ((ROWS, HEAD_DIM), BF),
        ((ROWS, HEAD_DIM), BF),
        ((ROWS, 1), F32),
        ((ROWS, HEAD_DIM), F32),
        ((ROWS, WINDOW + TOK), F32),
        ((ROWS, WINDOW + TOK), BF),
        ((ROWS, WINDOW + TOK), BF),
    ]
    return call(
        functools.partial(attend, g, len(earlier)),
        "attend",
        [((TOK, 2 * HALF), BF)] * RING
        + [((ROWS, 2 * HEAD_DIM), F32)]
        + [((ROWS, width), BF)] * 2,
        (pos, qseg, kseg, *qin, *kvs, *earlier),
        [pltpu.VMEM(shape, dtype) for shape, dtype in scratch],
        flops=6 * 2 * 4 * ROWS * 1152 * 256,
        limit=40,
    )


def columns(index, width):
    return pl.ds(pl.multiple_of(index * width, width), width)


def run_copies(pairs, sem):
    copies = [pltpu.make_async_copy(src, dst, sem.at[i]) for i, (src, dst) in enumerate(pairs)]
    for copy in copies:
        copy.start()
    for copy in copies:
        copy.wait()


def pack_kv(here_ref, k_ref, v_ref, *refs):
    outs, sem = refs[:RING], refs[RING]
    pairs = []
    for d in range(RING):
        for g in range(KV):
            cols = columns(jnp.bitwise_xor(here_ref[0], d) * KV + g, HEAD_DIM)
            for ref, base in ((k_ref, 0), (v_ref, HEAD_DIM)):
                at = 2 * g * HEAD_DIM + base
                pairs.append((ref.at[:, cols], outs[d].at[:, at : at + HEAD_DIM]))
    run_copies(pairs, sem)


def pack_q(here_ref, q_ref, d_ref, *refs):
    outs, sem = refs[: KV * RING], refs[KV * RING]
    pairs = []
    for g in range(KV):
        for d in range(RING):
            cols = columns(jnp.bitwise_xor(here_ref[0], d) * KV + g, HALF)
            for ref, base in ((q_ref, 0), (d_ref, HALF)):
                pairs.append((ref.at[:, cols], outs[g * RING + d].at[:, base : base + HALF]))
    run_copies(pairs, sem)


def add_kv(own0, own1, one, two, *outs):
    for g, own in enumerate((own0, own1)):
        cols = slice(2 * HEAD_DIM * g, 2 * HEAD_DIM * (g + 1))
        for d in range(RING):
            rows = slice(TOK * d, TOK * (d + 1))
            total = own[rows] + one[rows, cols].astype(F32) + two[rows, cols].astype(F32)
            outs[d][:, cols] = total.astype(BF)


def place_wide(g, here_ref, parts, attn, gq, sem):
    copies = []
    for d in range(RING):
        cols = columns(jnp.bitwise_xor(here_ref[0], d) * KV + g, HALF)
        for dst, base in ((attn, 0), (gq, HALF)):
            src = parts[d].at[:, base : base + HALF]
            copies.append(pltpu.make_async_copy(src, dst.at[:, cols], sem.at[len(copies)]))
    return copies


def assemble_first(here_ref, *refs):
    parts, (attn, gq, sem) = refs[:RING], refs[RING:]
    copies = place_wide(0, here_ref, parts, attn, gq, sem)
    for copy in copies:
        copy.start()
    for copy in copies:
        copy.wait()


def assemble(here_ref, *refs):
    parts, kvs = refs[2 : 2 + RING], refs[2 + RING : 2 + 2 * RING]
    attn, gq, gk, gv, sem = refs[2 + 2 * RING :]
    copies = place_wide(1, here_ref, parts, attn, gq, sem)
    for d in range(RING):
        for g in range(KV):
            cols = columns(jnp.bitwise_xor(here_ref[0], d) * KV + g, HEAD_DIM)
            for dst, base in ((gk, 2 * g * HEAD_DIM), (gv, (2 * g + 1) * HEAD_DIM)):
                src = kvs[d].at[:, base : base + HEAD_DIM]
                copies.append(pltpu.make_async_copy(src, dst.at[:, cols], sem.at[len(copies)]))
    for copy in copies:
        copy.start()
    for copy in copies:
        copy.wait()


def shards(queries, key_states, value_states, grad_output, segment_ids):
    heads = lax.axis_size("head")
    halves = lax.axis_size("blk") * heads // RING
    head = lax.axis_index("head")
    index = head % RING
    here = jnp.full((1,), index, jnp.int32)
    half = (lax.axis_index("blk") * heads + head) // RING

    def along_ring(value, d):
        return lax.ppermute(value, "head", [(i, i ^ d) for i in range(heads)])

    def along_halves(value, steps):
        pairs = [
            (i * RING + x, (i + steps) * RING + x)
            for i in range(max(0, -steps), min(halves, halves - steps))
            for x in range(RING)
        ]
        return lax.ppermute(value, ("blk", "head"), pairs)

    def around(parts):
        return parts[:1] + [along_ring(parts[d], d) for d in range(1, RING)]

    thin_part, wide_part = ((TOK, 2 * KV * HEAD_DIM), BF), ((TOK, 2 * HALF), BF)
    sems = [pltpu.SemaphoreType.DMA((2 * KV * RING,))]
    kv = call(
        pack_kv,
        "pack_kv",
        [thin_part] * RING,
        (here, key_states, value_states),
        sems,
        raw=True,
    )
    packed = call(
        pack_q,
        "pack_q",
        [wide_part] * (KV * RING),
        (here, queries, grad_output),
        sems,
        raw=True,
    )
    kv = around(kv)
    first, second = around(packed[:RING]), packed[RING:]
    kvs = []
    for g in range(KV):
        cols = slice(2 * HEAD_DIM * g, 2 * HEAD_DIM * (g + 1))
        own = jnp.concatenate([part[:, cols] for part in kv], axis=0)
        kvs.append((own, along_halves(own, 1), along_halves(own, 2)))
    second, _ = lax.optimization_barrier((second, kvs[0][0]))
    q_parts = (first, around(second))

    padded = jnp.concatenate([jnp.full((WINDOW,), HEAD_DIM - 1, jnp.int32), segment_ids])
    key_seg = lax.dynamic_slice_in_dim(padded, half * ROWS, EXT)
    lanes = jnp.arange(HEAD_DIM, dtype=jnp.int32)[None, :]
    kseg = (key_seg[:, None] == lanes).astype(BF)
    qseg = jnp.where(key_seg[WINDOW:, None] == lanes, 0.0, -BIG).astype(BF)
    steps = jnp.arange(RING, dtype=jnp.int32)
    pos = index ^ steps

    width = RING * KV * HALF
    wide_out, thin_out = ((TOK, width), BF), ((TOK, width // GROUP), BF)
    res0 = attend_call(0, pos, qseg, kseg, q_parts[0], kvs[0])
    wide0 = around(res0[:RING])
    res1 = attend_call(1, pos, qseg, kseg, q_parts[1], kvs[1], res0[5:])
    one, two = along_halves(res1[5], -1), along_halves(res1[6], -2)
    last, wide0 = lax.optimization_barrier((res1[:RING], wide0))
    wide1 = around(last)
    placed = call(
        assemble_first,
        "assemble_first",
        [wide_out] * 2,
        (here, *wide0),
        [pltpu.SemaphoreType.DMA((2 * RING,))],
        limit=16,
        space=pl.ANY,
    )
    grads = call(add_kv, "add_kv", [thin_part] * RING, (res0[4], res1[4], one, two), limit=16)
    grads = around(grads)
    return tuple(
        call(
            assemble,
            "assemble",
            [wide_out] * 2 + [thin_out] * 2,
            (here, *placed, *wide1, *grads),
            [pltpu.SemaphoreType.DMA((6 * RING,))],
            limit=16,
            space=pl.ANY,
            aliases={1: 0, 2: 1},
        )
    )


def solution(mesh):
    placed = P(("blk", "head"), None)
    return jax.shard_map(
        shards,
        mesh=mesh,
        in_specs=(placed, placed, placed, placed, P()),
        out_specs=(placed, placed, placed, placed),
        check_vma=False,
    )
```

```python
import functools
import math

import jax
import jax.numpy as jnp
from jax import lax
from jax.experimental import pallas as pl
from jax.experimental.pallas import tpu as pltpu
from jax.sharding import PartitionSpec as P

HEAD_DIM = 128
WINDOW = 1024
RING = 4
TOK = 128
ROWS = RING * TOK
GROUP = 4
KV = 2
HALF = GROUP * HEAD_DIM
EXT = ROWS + WINDOW
SCALE = 1.0 / math.sqrt(HEAD_DIM)
LOG2E = math.log2(math.e)
BIG = 16384.0
BF = jnp.bfloat16
F32 = jnp.float32
NT = (((1,), (1,)), ((), ()))
TN = (((0,), (0,)), ((), ()))


def attend(g, n_earlier, pos_ref, qseg_ref, kseg_ref, *refs):
    qin, (kvo, kv1, kv2) = refs[:4], refs[4:7]
    earlier, refs = refs[7 : 7 + n_earlier], refs[7 + n_earlier :]
    outs, (dko, dk1, dk2) = refs[:4], refs[4:7]
    kx, vx, acck, accv, qs, dos, qn, gn, dots, invs, s_scr, p_scr, d_scr = refs[7:]

    for src, base in ((kv2, 0), (kv1, ROWS), (kvo, 2 * ROWS)):
        for d in range(RING):
            row = pl.ds(pl.multiple_of(base + TOK * pos_ref[d], TOK), TOK)
            kx[row, :HEAD_DIM] = src[TOK * d : TOK * (d + 1), :HEAD_DIM]
            vx[row, :HEAD_DIM] = src[TOK * d : TOK * (d + 1), HEAD_DIM:]
    kx[:, HEAD_DIM:] = kseg_ref[...]
    vx[:, HEAD_DIM:] = jnp.ones((EXT, HEAD_DIM), BF)
    acck[...] = jnp.zeros_like(acck)
    accv[...] = jnp.zeros_like(accv)
    for d in range(RING):
        seg = qseg_ref[pl.ds(pl.multiple_of(TOK * pos_ref[d], TOK), TOK)]
        for j in range(GROUP):
            sl = slice(TOK * j, TOK * (j + 1))
            qs[d, sl, :HEAD_DIM] = qin[d][:, HEAD_DIM * j : HEAD_DIM * (j + 1)]
            qs[d, sl, HEAD_DIM:] = seg
            dos[d, sl] = qin[d][:, HALF + HEAD_DIM * j : HALF + HEAD_DIM * (j + 1)]

    row_id = lax.broadcasted_iota(jnp.int32, (TOK, TOK), 0)
    col_id = lax.broadcasted_iota(jnp.int32, (TOK, TOK), 1)
    lower = col_id <= row_id

    def put(ref, row, base, value):
        for i in range(value.shape[0] // TOK):
            at = base + (row // TOK + i) * HEAD_DIM
            ref[:, at : at + HEAD_DIM] = value[TOK * i : TOK * (i + 1)]

    def step(d, carry):
        start = pl.multiple_of(TOK * pos_ref[d], TOK)
        span = pl.ds(start, WINDOW + TOK)
        s_scr[...] = lax.dot_general(qs[d], kx[span], NT, preferred_element_type=F32)
        for j in range(GROUP):
            sl = slice(TOK * j, TOK * (j + 1))
            edge = jnp.where(lower, s_scr[sl, WINDOW:], s_scr[sl, :TOK])
            body = s_scr[sl, TOK:WINDOW]
            top = jnp.maximum(
                jnp.max(edge, axis=1, keepdims=True), jnp.max(body, axis=1, keepdims=True)
            )
            edge = jnp.exp2((edge - top) * (SCALE * LOG2E))
            p_scr[sl, :TOK] = jnp.where(lower, 0.0, edge).astype(BF)
            p_scr[sl, WINDOW:] = jnp.where(lower, edge, 0.0).astype(BF)
            p_scr[sl, TOK:WINDOW] = jnp.exp2((body - top) * (SCALE * LOG2E)).astype(BF)
        for j in range(0, ROWS, 256):
            sl = slice(j, j + 256)
            out = jnp.dot(p_scr[sl], vx[span], preferred_element_type=F32)
            inv = 1.0 / out[:, HEAD_DIM:]
            attn = (out[:, :HEAD_DIM] * inv).astype(BF)
            put(outs[d], j, 0, attn)
            grad = dos[d, sl].astype(F32)
            dots[sl] = jnp.sum(grad * attn.astype(F32), axis=1, keepdims=True)
            invs[sl] = inv * SCALE
            qn[sl] = (qs[d, sl, :HEAD_DIM].astype(F32) * (inv * SCALE)).astype(BF)
            gn[sl] = (grad * inv).astype(BF)
        d_scr[...] = (
            (lax.dot_general(dos[d], vx[span, :HEAD_DIM], NT, preferred_element_type=F32) - dots[...])
            * p_scr[...].astype(F32)
        ).astype(BF)
        for j in range(0, ROWS, 256):
            sl = slice(j, j + 256)
            dq = jnp.dot(d_scr[sl], kx[span, :HEAD_DIM], preferred_element_type=F32)
            put(outs[d], j, HALF, (dq * invs[sl]).astype(BF))
        acck[:, span] += lax.dot_general(qn[...], d_scr[...], TN, preferred_element_type=F32)
        accv[:, span] += lax.dot_general(gn[...], p_scr[...], TN, preferred_element_type=F32)
        return carry

    for d in range(RING):
        step(d, 0)

    for dst, src in zip((dk1, dk2), earlier):
        dst[:, : src.shape[1]] = src[...]
    for dst, base in ((dk2, 0), (dk1, ROWS), (dko, 2 * ROWS)):
        at = dst.shape[1] - 2 * HEAD_DIM
        for d in range(RING):
            row = pl.ds(pl.multiple_of(base + TOK * pos_ref[d], TOK), TOK)
            sl = slice(TOK * d, TOK * (d + 1))
            dst[sl, at : at + HEAD_DIM] = acck[:, row].T.astype(dst.dtype)
            dst[sl, at + HEAD_DIM :] = accv[:, row].T.astype(dst.dtype)


def call(
    body,
    name,
    shapes,
    args,
    scratch=(),
    flops=0,
    limit=60,
    space=pltpu.VMEM,
    aliases=None,
    raw=False,
):
    at = pl.BlockSpec(memory_space=space)
    vm = pl.BlockSpec(memory_space=pltpu.VMEM)
    hbm = pl.BlockSpec(memory_space=pl.ANY)
    sm = pl.BlockSpec(memory_space=pltpu.SMEM)
    return list(
        pl.pallas_call(
            body,
            out_shape=[jax.ShapeDtypeStruct(shape, dtype) for shape, dtype in shapes],
            in_specs=[
                sm if arg.ndim == 1 else hbm if raw or i in (aliases or {}) else vm
                for i, arg in enumerate(args)
            ],
            out_specs=[at] * len(shapes),
            scratch_shapes=list(scratch),
            input_output_aliases=aliases or {},
            compiler_params=pltpu.CompilerParams(vmem_limit_bytes=limit * 1024 * 1024),
            cost_estimate=pl.CostEstimate(
                flops=flops, bytes_accessed=4 * 1024 * 1024, transcendentals=0
            ),
            name=name,
        )(*args)
    )


def attend_call(g, pos, qseg, kseg, qin, kvs, earlier=()):
    width = 2 * HEAD_DIM * (g + 1)
    scratch = [
        ((EXT, 2 * HEAD_DIM), BF),
        ((EXT, 2 * HEAD_DIM), BF),
        ((HEAD_DIM, EXT), F32),
        ((HEAD_DIM, EXT), F32),
        ((RING, ROWS, 2 * HEAD_DIM), BF),
        ((RING, ROWS, HEAD_DIM), BF),
        ((ROWS, HEAD_DIM), BF),
        ((ROWS, HEAD_DIM), BF),
        ((ROWS, 1), F32),
        ((ROWS, HEAD_DIM), F32),
        ((ROWS, WINDOW + TOK), F32),
        ((ROWS, WINDOW + TOK), BF),
        ((ROWS, WINDOW + TOK), BF),
    ]
    return call(
        functools.partial(attend, g, len(earlier)),
        "attend",
        [((TOK, 2 * HALF), BF)] * RING
        + [((ROWS, 2 * HEAD_DIM), F32)]
        + [((ROWS, width), BF)] * 2,
        (pos, qseg, kseg, *qin, *kvs, *earlier),
        [pltpu.VMEM(shape, dtype) for shape, dtype in scratch],
        flops=6 * 2 * 4 * ROWS * 1152 * 256,
        limit=40,
    )


def columns(index, width):
    return pl.ds(pl.multiple_of(index * width, width), width)


def run_copies(pairs, sem):
    copies = [pltpu.make_async_copy(src, dst, sem.at[i]) for i, (src, dst) in enumerate(pairs)]
    for copy in copies:
        copy.start()
    for copy in copies:
        copy.wait()


def pack_kv(here_ref, k_ref, v_ref, *refs):
    outs, sem = refs[:RING], refs[RING]
    pairs = []
    for d in range(RING):
        for g in range(KV):
            cols = columns(jnp.bitwise_xor(here_ref[0], d) * KV + g, HEAD_DIM)
            for ref, base in ((k_ref, 0), (v_ref, HEAD_DIM)):
                at = 2 * g * HEAD_DIM + base
                pairs.append((ref.at[:, cols], outs[d].at[:, at : at + HEAD_DIM]))
    run_copies(pairs, sem)


def pack_q(here_ref, q_ref, d_ref, *refs):
    outs, sem = refs[: KV * RING], refs[KV * RING]
    pairs = []
    for g in range(KV):
        for d in range(RING):
            cols = columns(jnp.bitwise_xor(here_ref[0], d) * KV + g, HALF)
            for ref, base in ((q_ref, 0), (d_ref, HALF)):
                pairs.append((ref.at[:, cols], outs[g * RING + d].at[:, base : base + HALF]))
    run_copies(pairs, sem)


def add_kv(own0, own1, one, two, *outs):
    for g, own in enumerate((own0, own1)):
        cols = slice(2 * HEAD_DIM * g, 2 * HEAD_DIM * (g + 1))
        for d in range(RING):
            rows = slice(TOK * d, TOK * (d + 1))
            total = own[rows] + one[rows, cols].astype(F32) + two[rows, cols].astype(F32)
            outs[d][:, cols] = total.astype(BF)


def place_wide(g, here_ref, parts, attn, gq, sem):
    copies = []
    for d in range(RING):
        cols = columns(jnp.bitwise_xor(here_ref[0], d) * KV + g, HALF)
        for dst, base in ((attn, 0), (gq, HALF)):
            src = parts[d].at[:, base : base + HALF]
            copies.append(pltpu.make_async_copy(src, dst.at[:, cols], sem.at[len(copies)]))
    return copies


def assemble_first(here_ref, *refs):
    parts, (attn, gq, sem) = refs[:RING], refs[RING:]
    copies = place_wide(0, here_ref, parts, attn, gq, sem)
    for copy in copies:
        copy.start()
    for copy in copies:
        copy.wait()


def assemble(here_ref, *refs):
    parts, kvs = refs[2 : 2 + RING], refs[2 + RING : 2 + 2 * RING]
    attn, gq, gk, gv, sem = refs[2 + 2 * RING :]
    copies = place_wide(1, here_ref, parts, attn, gq, sem)
    for d in range(RING):
        for g in range(KV):
            cols = columns(jnp.bitwise_xor(here_ref[0], d) * KV + g, HEAD_DIM)
            for dst, base in ((gk, 2 * g * HEAD_DIM), (gv, (2 * g + 1) * HEAD_DIM)):
                src = kvs[d].at[:, base : base + HEAD_DIM]
                copies.append(pltpu.make_async_copy(src, dst.at[:, cols], sem.at[len(copies)]))
    for copy in copies:
        copy.start()
    for copy in copies:
        copy.wait()


def shards(queries, key_states, value_states, grad_output, segment_ids):
    heads = lax.axis_size("head")
    halves = lax.axis_size("blk") * heads // RING
    head = lax.axis_index("head")
    index = head % RING
    here = jnp.full((1,), index, jnp.int32)
    half = (lax.axis_index("blk") * heads + head) // RING

    def along_ring(value, d):
        return lax.ppermute(value, "head", [(i, i ^ d) for i in range(heads)])

    def along_halves(value, steps):
        count = halves * RING
        pairs = [(i, (i + steps * RING) % count) for i in range(count)]
        return lax.ppermute(value, ("blk", "head"), pairs)

    def around(parts):
        return parts[:1] + [along_ring(parts[d], d) for d in range(1, RING)]

    thin_part, wide_part = ((TOK, 2 * KV * HEAD_DIM), BF), ((TOK, 2 * HALF), BF)
    sems = [pltpu.SemaphoreType.DMA((2 * KV * RING,))]
    kv = call(
        pack_kv,
        "pack_kv",
        [thin_part] * RING,
        (here, key_states, value_states),
        sems,
        raw=True,
    )
    packed = call(
        pack_q,
        "pack_q",
        [wide_part] * (KV * RING),
        (here, queries, grad_output),
        sems,
        raw=True,
    )
    kv = around(kv)
    first, second = around(packed[:RING]), packed[RING:]
    kvs = []
    for g in range(KV):
        cols = slice(2 * HEAD_DIM * g, 2 * HEAD_DIM * (g + 1))
        own = jnp.concatenate([part[:, cols] for part in kv], axis=0)
        kvs.append((own, along_halves(own, 1), along_halves(own, 2)))
    second, _ = lax.optimization_barrier((second, kvs[0][0]))
    q_parts = (first, around(second))

    padded = jnp.concatenate([jnp.full((WINDOW,), HEAD_DIM - 1, jnp.int32), segment_ids])
    key_seg = lax.dynamic_slice_in_dim(padded, half * ROWS, EXT)
    lanes = jnp.arange(HEAD_DIM, dtype=jnp.int32)[None, :]
    kseg = (key_seg[:, None] == lanes).astype(BF)
    qseg = jnp.where(key_seg[WINDOW:, None] == lanes, 0.0, -BIG).astype(BF)
    steps = jnp.arange(RING, dtype=jnp.int32)
    pos = index ^ steps

    width = RING * KV * HALF
    wide_out, thin_out = ((TOK, width), BF), ((TOK, width // GROUP), BF)
    res0 = attend_call(0, pos, qseg, kseg, q_parts[0], kvs[0])
    wide0 = around(res0[:RING])
    res1 = attend_call(1, pos, qseg, kseg, q_parts[1], kvs[1], res0[5:])
    one, two = along_halves(res1[5], -1), along_halves(res1[6], -2)
    last, wide0 = lax.optimization_barrier((res1[:RING], wide0))
    wide1 = around(last)
    placed = call(
        assemble_first,
        "assemble_first",
        [wide_out] * 2,
        (here, *wide0),
        [pltpu.SemaphoreType.DMA((2 * RING,))],
        limit=16,
        space=pl.ANY,
    )
    grads = call(add_kv, "add_kv", [thin_part] * RING, (res0[4], res1[4], one, two), limit=16)
    grads = around(grads)
    return tuple(
        call(
            assemble,
            "assemble",
            [wide_out] * 2 + [thin_out] * 2,
            (here, *placed, *wide1, *grads),
            [pltpu.SemaphoreType.DMA((6 * RING,))],
            limit=16,
            space=pl.ANY,
            aliases={1: 0, 2: 1},
        )
    )


def solution(mesh):
    placed = P(("blk", "head"), None)
    return jax.shard_map(
        shards,
        mesh=mesh,
        in_specs=(placed, placed, placed, placed, P()),
        out_specs=(placed, placed, placed, placed),
        check_vma=False,
    )
```

```python
import functools
import math

import jax
import jax.numpy as jnp
from jax import lax
from jax.experimental import pallas as pl
from jax.experimental.pallas import tpu as pltpu
from jax.sharding import PartitionSpec as P

HEAD_DIM = 128
WINDOW = 1024
RING = 4
TOK = 128
ROWS = RING * TOK
GROUP = 4
KV = 2
HALF = GROUP * HEAD_DIM
EXT = ROWS + WINDOW
SCALE = 1.0 / math.sqrt(HEAD_DIM)
LOG2E = math.log2(math.e)
BIG = 16384.0
BF = jnp.bfloat16
F32 = jnp.float32
NT = (((1,), (1,)), ((), ()))
TN = (((0,), (0,)), ((), ()))


def attend(pos_ref, qseg_ref, kseg_ref, *refs):
    qin, (kvo, kv1, kv2) = refs[:4], refs[4:7]
    refs = refs[7:]
    outs, (dko, dk1, dk2) = refs[:4], refs[4:7]
    kx, vx, acck, accv, qs, dos, qn, gn, dots, invs, s_scr, p_scr, d_scr = refs[7:]

    for src, base in ((kv2, 0), (kv1, ROWS), (kvo, 2 * ROWS)):
        for d in range(RING):
            row = pl.ds(pl.multiple_of(base + TOK * pos_ref[d], TOK), TOK)
            kx[row, :HEAD_DIM] = src[TOK * d : TOK * (d + 1), :HEAD_DIM]
            vx[row, :HEAD_DIM] = src[TOK * d : TOK * (d + 1), HEAD_DIM:]
    kx[:, HEAD_DIM:] = kseg_ref[...]
    vx[:, HEAD_DIM:] = jnp.ones((EXT, HEAD_DIM), BF)
    acck[...] = jnp.zeros_like(acck)
    accv[...] = jnp.zeros_like(accv)
    for d in range(RING):
        seg = qseg_ref[pl.ds(pl.multiple_of(TOK * pos_ref[d], TOK), TOK)]
        for j in range(GROUP):
            sl = slice(TOK * j, TOK * (j + 1))
            qs[d, sl, :HEAD_DIM] = qin[d][:, HEAD_DIM * j : HEAD_DIM * (j + 1)]
            qs[d, sl, HEAD_DIM:] = seg
            dos[d, sl] = qin[d][:, HALF + HEAD_DIM * j : HALF + HEAD_DIM * (j + 1)]

    row_id = lax.broadcasted_iota(jnp.int32, (TOK, TOK), 0)
    col_id = lax.broadcasted_iota(jnp.int32, (TOK, TOK), 1)
    lower = col_id <= row_id

    def put(ref, row, base, value):
        for i in range(value.shape[0] // TOK):
            at = base + (row // TOK + i) * HEAD_DIM
            ref[:, at : at + HEAD_DIM] = value[TOK * i : TOK * (i + 1)]

    def step(d, carry):
        start = pl.multiple_of(TOK * pos_ref[d], TOK)
        span = pl.ds(start, WINDOW + TOK)
        s_scr[...] = lax.dot_general(qs[d], kx[span], NT, preferred_element_type=F32)
        for j in range(GROUP):
            sl = slice(TOK * j, TOK * (j + 1))
            edge = jnp.where(lower, s_scr[sl, WINDOW:], s_scr[sl, :TOK])
            body = s_scr[sl, TOK:WINDOW]
            top = jnp.maximum(
                jnp.max(edge, axis=1, keepdims=True), jnp.max(body, axis=1, keepdims=True)
            )
            edge = jnp.exp2((edge - top) * (SCALE * LOG2E))
            p_scr[sl, :TOK] = jnp.where(lower, 0.0, edge).astype(BF)
            p_scr[sl, WINDOW:] = jnp.where(lower, edge, 0.0).astype(BF)
            p_scr[sl, TOK:WINDOW] = jnp.exp2((body - top) * (SCALE * LOG2E)).astype(BF)
        for j in range(0, ROWS, 256):
            sl = slice(j, j + 256)
            out = jnp.dot(p_scr[sl], vx[span], preferred_element_type=F32)
            inv = 1.0 / out[:, HEAD_DIM:]
            attn = (out[:, :HEAD_DIM] * inv).astype(BF)
            put(outs[d], j, 0, attn)
            grad = dos[d, sl].astype(F32)
            dots[sl] = jnp.sum(grad * attn.astype(F32), axis=1, keepdims=True)
            invs[sl] = inv * SCALE
            qn[sl] = (qs[d, sl, :HEAD_DIM].astype(F32) * (inv * SCALE)).astype(BF)
            gn[sl] = (grad * inv).astype(BF)
        d_scr[...] = (
            (lax.dot_general(dos[d], vx[span, :HEAD_DIM], NT, preferred_element_type=F32) - dots[...])
            * p_scr[...].astype(F32)
        ).astype(BF)
        for j in range(0, ROWS, 256):
            sl = slice(j, j + 256)
            dq = jnp.dot(d_scr[sl], kx[span, :HEAD_DIM], preferred_element_type=F32)
            put(outs[d], j, HALF, (dq * invs[sl]).astype(BF))
        acck[:, span] += lax.dot_general(qn[...], d_scr[...], TN, preferred_element_type=F32)
        accv[:, span] += lax.dot_general(gn[...], p_scr[...], TN, preferred_element_type=F32)
        return carry

    for d in range(RING):
        step(d, 0)

    for dst, base in ((dk2, 0), (dk1, ROWS), (dko, 2 * ROWS)):
        for d in range(RING):
            row = pl.ds(pl.multiple_of(base + TOK * pos_ref[d], TOK), TOK)
            sl = slice(TOK * d, TOK * (d + 1))
            dst[sl, :HEAD_DIM] = acck[:, row].T.astype(dst.dtype)
            dst[sl, HEAD_DIM:] = accv[:, row].T.astype(dst.dtype)


def call(
    body,
    name,
    shapes,
    args,
    scratch=(),
    flops=0,
    limit=60,
    space=pltpu.VMEM,
    aliases=None,
    raw=False,
):
    at = pl.BlockSpec(memory_space=space)
    vm = pl.BlockSpec(memory_space=pltpu.VMEM)
    hbm = pl.BlockSpec(memory_space=pl.ANY)
    sm = pl.BlockSpec(memory_space=pltpu.SMEM)
    return list(
        pl.pallas_call(
            body,
            out_shape=[jax.ShapeDtypeStruct(shape, dtype) for shape, dtype in shapes],
            in_specs=[
                sm if arg.ndim == 1 else hbm if raw or i in (aliases or {}) else vm
                for i, arg in enumerate(args)
            ],
            out_specs=[at] * len(shapes),
            scratch_shapes=list(scratch),
            input_output_aliases=aliases or {},
            compiler_params=pltpu.CompilerParams(vmem_limit_bytes=limit * 1024 * 1024),
            cost_estimate=pl.CostEstimate(
                flops=flops, bytes_accessed=4 * 1024 * 1024, transcendentals=0
            ),
            name=name,
        )(*args)
    )


def attend_call(pos, qseg, kseg, qin, kvs):
    scratch = [
        ((EXT, 2 * HEAD_DIM), BF),
        ((EXT, 2 * HEAD_DIM), BF),
        ((HEAD_DIM, EXT), F32),
        ((HEAD_DIM, EXT), F32),
        ((RING, ROWS, 2 * HEAD_DIM), BF),
        ((RING, ROWS, HEAD_DIM), BF),
        ((ROWS, HEAD_DIM), BF),
        ((ROWS, HEAD_DIM), BF),
        ((ROWS, 1), F32),
        ((ROWS, HEAD_DIM), F32),
        ((ROWS, WINDOW + TOK), F32),
        ((ROWS, WINDOW + TOK), BF),
        ((ROWS, WINDOW + TOK), BF),
    ]
    return call(
        attend,
        "attend",
        [((TOK, 2 * HALF), BF)] * RING
        + [((ROWS, 2 * HEAD_DIM), F32)]
        + [((ROWS, 2 * HEAD_DIM), BF)] * 2,
        (pos, qseg, kseg, *qin, *kvs),
        [pltpu.VMEM(shape, dtype) for shape, dtype in scratch],
        flops=6 * 2 * 4 * ROWS * 1152 * 256,
        limit=40,
    )


def columns(index, width):
    return pl.ds(pl.multiple_of(index * width, width), width)


def run_copies(pairs, sem):
    copies = [pltpu.make_async_copy(src, dst, sem.at[i]) for i, (src, dst) in enumerate(pairs)]
    for copy in copies:
        copy.start()
    for copy in copies:
        copy.wait()


def pack_kv(here_ref, k_ref, v_ref, *refs):
    outs, sem = refs[:RING], refs[RING]
    pairs = []
    for d in range(RING):
        for g in range(KV):
            cols = columns(jnp.bitwise_xor(here_ref[0], d) * KV + g, HEAD_DIM)
            for ref, base in ((k_ref, 0), (v_ref, HEAD_DIM)):
                at = 2 * g * HEAD_DIM + base
                pairs.append((ref.at[:, cols], outs[d].at[:, at : at + HEAD_DIM]))
    run_copies(pairs, sem)


def pack_q(g, here_ref, q_ref, d_ref, *refs):
    outs, sem = refs[:RING], refs[RING]
    pairs = []
    for d in range(RING):
        cols = columns(jnp.bitwise_xor(here_ref[0], d) * KV + g, HALF)
        for ref, base in ((q_ref, 0), (d_ref, HALF)):
            pairs.append((ref.at[:, cols], outs[d].at[:, base : base + HALF]))
    run_copies(pairs, sem)


def add_kv(own0, own1, one0, two0, one1, two1, *outs):
    for g, (own, one, two) in enumerate(((own0, one0, two0), (own1, one1, two1))):
        cols = slice(2 * HEAD_DIM * g, 2 * HEAD_DIM * (g + 1))
        for d in range(RING):
            rows = slice(TOK * d, TOK * (d + 1))
            total = own[rows] + one[rows].astype(F32) + two[rows].astype(F32)
            outs[d][:, cols] = total.astype(BF)


def place_wide(g, here_ref, parts, attn, gq, sem):
    copies = []
    for d in range(RING):
        cols = columns(jnp.bitwise_xor(here_ref[0], d) * KV + g, HALF)
        for dst, base in ((attn, 0), (gq, HALF)):
            src = parts[d].at[:, base : base + HALF]
            copies.append(pltpu.make_async_copy(src, dst.at[:, cols], sem.at[len(copies)]))
    return copies


def assemble_first(here_ref, *refs):
    parts, (attn, gq, sem) = refs[:RING], refs[RING:]
    copies = place_wide(0, here_ref, parts, attn, gq, sem)
    for copy in copies:
        copy.start()
    for copy in copies:
        copy.wait()


def assemble(here_ref, *refs):
    parts, kvs = refs[2 : 2 + RING], refs[2 + RING : 2 + 2 * RING]
    attn, gq, gk, gv, sem = refs[2 + 2 * RING :]
    copies = place_wide(1, here_ref, parts, attn, gq, sem)
    for d in range(RING):
        for g in range(KV):
            cols = columns(jnp.bitwise_xor(here_ref[0], d) * KV + g, HEAD_DIM)
            for dst, base in ((gk, 2 * g * HEAD_DIM), (gv, (2 * g + 1) * HEAD_DIM)):
                src = kvs[d].at[:, base : base + HEAD_DIM]
                copies.append(pltpu.make_async_copy(src, dst.at[:, cols], sem.at[len(copies)]))
    for copy in copies:
        copy.start()
    for copy in copies:
        copy.wait()


def shards(queries, key_states, value_states, grad_output, segment_ids):
    heads = lax.axis_size("head")
    halves = lax.axis_size("blk") * heads // RING
    head = lax.axis_index("head")
    index = head % RING
    here = jnp.full((1,), index, jnp.int32)
    half = (lax.axis_index("blk") * heads + head) // RING

    def along_ring(value, d):
        return lax.ppermute(value, "head", [(i, i ^ d) for i in range(heads)])

    def along_halves(value, steps):
        count = halves * RING
        pairs = [(i, (i + steps * RING) % count) for i in range(count)]
        return lax.ppermute(value, ("blk", "head"), pairs)

    def around(parts):
        return parts[:1] + [along_ring(parts[d], d) for d in range(1, RING)]

    thin_part, wide_part = ((TOK, 2 * KV * HEAD_DIM), BF), ((TOK, 2 * HALF), BF)
    sems = [pltpu.SemaphoreType.DMA((2 * KV * RING,))]
    kv = call(
        pack_kv,
        "pack_kv",
        [thin_part] * RING,
        (here, key_states, value_states),
        sems,
        raw=True,
    )

    def pack(g, q, do):
        return call(
            functools.partial(pack_q, g),
            "pack_q",
            [wide_part] * RING,
            (here, q, do),
            sems,
            raw=True,
        )

    kv = around(kv)
    first = around(pack(0, queries, grad_output))
    kvs = []
    for g in range(KV):
        cols = slice(2 * HEAD_DIM * g, 2 * HEAD_DIM * (g + 1))
        own = jnp.concatenate([part[:, cols] for part in kv], axis=0)
        kvs.append((own, along_halves(own, 1), along_halves(own, 2)))
    late, _ = lax.optimization_barrier(((queries, grad_output), kvs[0][0]))
    q_parts = (first, around(pack(1, *late)))

    padded = jnp.concatenate([jnp.full((WINDOW,), HEAD_DIM - 1, jnp.int32), segment_ids])
    key_seg = lax.dynamic_slice_in_dim(padded, half * ROWS, EXT)
    lanes = jnp.arange(HEAD_DIM, dtype=jnp.int32)[None, :]
    kseg = (key_seg[:, None] == lanes).astype(BF)
    qseg = jnp.where(key_seg[WINDOW:, None] == lanes, 0.0, -BIG).astype(BF)
    steps = jnp.arange(RING, dtype=jnp.int32)
    pos = index ^ steps

    width = RING * KV * HALF
    wide_out, thin_out = ((TOK, width), BF), ((TOK, width // GROUP), BF)
    res0 = attend_call(pos, qseg, kseg, q_parts[0], kvs[0])
    wide0 = around(res0[:RING])
    back0 = [along_halves(res0[5], -1), along_halves(res0[6], -2)]
    res1 = attend_call(pos, qseg, kseg, q_parts[1], kvs[1])
    tail, back0 = lax.optimization_barrier((res1[5:], back0))
    back1 = [along_halves(tail[0], -1), along_halves(tail[1], -2)]
    last, wide0 = lax.optimization_barrier((res1[:RING], wide0))
    wide1 = around(last)
    placed = call(
        assemble_first,
        "assemble_first",
        [wide_out] * 2,
        (here, *wide0),
        [pltpu.SemaphoreType.DMA((2 * RING,))],
        limit=16,
        space=pl.ANY,
    )
    grads = call(add_kv, "add_kv", [thin_part] * RING, (res0[4], res1[4], *back0, *back1), limit=16)
    grads = around(grads)
    return tuple(
        call(
            assemble,
            "assemble",
            [wide_out] * 2 + [thin_out] * 2,
            (here, *placed, *wide1, *grads),
            [pltpu.SemaphoreType.DMA((6 * RING,))],
            limit=16,
            space=pl.ANY,
            aliases={1: 0, 2: 1},
        )
    )


def solution(mesh):
    placed = P(("blk", "head"), None)
    return jax.shard_map(
        shards,
        mesh=mesh,
        in_specs=(placed, placed, placed, placed, P()),
        out_specs=(placed, placed, placed, placed),
        check_vma=False,
    )
```

```python
import functools
import math

import jax
import jax.numpy as jnp
from jax import lax
from jax.experimental import pallas as pl
from jax.experimental.pallas import tpu as pltpu
from jax.sharding import PartitionSpec as P

HEAD_DIM = 128
WINDOW = 1024
RING = 4
TOK = 128
ROWS = RING * TOK
GROUP = 4
KV = 2
HALF = GROUP * HEAD_DIM
EXT = ROWS + WINDOW
SCALE = 1.0 / math.sqrt(HEAD_DIM)
LOG2E = math.log2(math.e)
BIG = 16384.0
BF = jnp.bfloat16
F32 = jnp.float32
NT = (((1,), (1,)), ((), ()))
TN = (((0,), (0,)), ((), ()))


def attend(g, n_earlier, pos_ref, qseg_ref, kseg_ref, *refs):
    qin, (kvo, kv1, kv2) = refs[:4], refs[4:7]
    earlier, refs = refs[7 : 7 + n_earlier], refs[7 + n_earlier :]
    outs, (dko, dk1, dk2) = refs[:4], refs[4:7]
    kx, vx, acck, accv, qs, dos, qn, gn, dots, invs, s_scr, p_scr, d_scr = refs[7:]

    for src, base in ((kv2, 0), (kv1, ROWS), (kvo, 2 * ROWS)):
        for d in range(RING):
            row = pl.ds(pl.multiple_of(base + TOK * pos_ref[d], TOK), TOK)
            kx[row, :HEAD_DIM] = src[TOK * d : TOK * (d + 1), :HEAD_DIM]
            vx[row, :HEAD_DIM] = src[TOK * d : TOK * (d + 1), HEAD_DIM:]
    kx[:, HEAD_DIM:] = kseg_ref[...]
    vx[:, HEAD_DIM:] = jnp.ones((EXT, HEAD_DIM), BF)
    acck[...] = jnp.zeros_like(acck)
    accv[...] = jnp.zeros_like(accv)
    for d in range(RING):
        seg = qseg_ref[pl.ds(pl.multiple_of(TOK * pos_ref[d], TOK), TOK)]
        for j in range(GROUP):
            sl = slice(TOK * j, TOK * (j + 1))
            qs[d, sl, :HEAD_DIM] = qin[d][:, HEAD_DIM * j : HEAD_DIM * (j + 1)]
            qs[d, sl, HEAD_DIM:] = seg
            dos[d, sl] = qin[d][:, HALF + HEAD_DIM * j : HALF + HEAD_DIM * (j + 1)]

    row_id = lax.broadcasted_iota(jnp.int32, (TOK, TOK), 0)
    col_id = lax.broadcasted_iota(jnp.int32, (TOK, TOK), 1)
    lower = col_id <= row_id

    def put(ref, row, base, value):
        for i in range(value.shape[0] // TOK):
            at = base + (row // TOK + i) * HEAD_DIM
            ref[:, at : at + HEAD_DIM] = value[TOK * i : TOK * (i + 1)]

    def step(d, carry):
        start = pl.multiple_of(TOK * pos_ref[d], TOK)
        span = pl.ds(start, WINDOW + TOK)
        s_scr[...] = lax.dot_general(qs[d], kx[span], NT, preferred_element_type=F32)
        for j in range(GROUP):
            sl = slice(TOK * j, TOK * (j + 1))
            edge = jnp.where(lower, s_scr[sl, WINDOW:], s_scr[sl, :TOK])
            body = s_scr[sl, TOK:WINDOW]
            top = jnp.maximum(
                jnp.max(edge, axis=1, keepdims=True), jnp.max(body, axis=1, keepdims=True)
            )
            edge = jnp.exp2((edge - top) * (SCALE * LOG2E))
            p_scr[sl, :TOK] = jnp.where(lower, 0.0, edge).astype(BF)
            p_scr[sl, WINDOW:] = jnp.where(lower, edge, 0.0).astype(BF)
            p_scr[sl, TOK:WINDOW] = jnp.exp2((body - top) * (SCALE * LOG2E)).astype(BF)
        for j in range(0, ROWS, 256):
            sl = slice(j, j + 256)
            out = jnp.dot(p_scr[sl], vx[span], preferred_element_type=F32)
            inv = 1.0 / out[:, HEAD_DIM:]
            attn = (out[:, :HEAD_DIM] * inv).astype(BF)
            put(outs[d], j, 0, attn)
            grad = dos[d, sl].astype(F32)
            dots[sl] = jnp.sum(grad * attn.astype(F32), axis=1, keepdims=True)
            invs[sl] = inv * SCALE
            qn[sl] = (qs[d, sl, :HEAD_DIM].astype(F32) * (inv * SCALE)).astype(BF)
            gn[sl] = (grad * inv).astype(BF)
        d_scr[...] = (
            (lax.dot_general(dos[d], vx[span, :HEAD_DIM], NT, preferred_element_type=F32) - dots[...])
            * p_scr[...].astype(F32)
        ).astype(BF)
        for j in range(0, ROWS, 256):
            sl = slice(j, j + 256)
            dq = jnp.dot(d_scr[sl], kx[span, :HEAD_DIM], preferred_element_type=F32)
            put(outs[d], j, HALF, (dq * invs[sl]).astype(BF))
        acck[:, span] += lax.dot_general(qn[...], d_scr[...], TN, preferred_element_type=F32)
        accv[:, span] += lax.dot_general(gn[...], p_scr[...], TN, preferred_element_type=F32)
        return carry

    for d in range(RING):
        step(d, 0)

    for dst, src in zip((dk1, dk2), earlier):
        dst[:, : src.shape[1]] = src[...]
    for dst, base in ((dk2, 0), (dk1, ROWS), (dko, 2 * ROWS)):
        at = dst.shape[1] - 2 * HEAD_DIM
        for d in range(RING):
            row = pl.ds(pl.multiple_of(base + TOK * pos_ref[d], TOK), TOK)
            sl = slice(TOK * d, TOK * (d + 1))
            dst[sl, at : at + HEAD_DIM] = acck[:, row].T.astype(dst.dtype)
            dst[sl, at + HEAD_DIM :] = accv[:, row].T.astype(dst.dtype)


def call(
    body,
    name,
    shapes,
    args,
    scratch=(),
    flops=0,
    limit=60,
    space=pltpu.VMEM,
    aliases=None,
    raw=False,
):
    at = pl.BlockSpec(memory_space=space)
    vm = pl.BlockSpec(memory_space=pltpu.VMEM)
    hbm = pl.BlockSpec(memory_space=pl.ANY)
    sm = pl.BlockSpec(memory_space=pltpu.SMEM)
    return list(
        pl.pallas_call(
            body,
            out_shape=[jax.ShapeDtypeStruct(shape, dtype) for shape, dtype in shapes],
            in_specs=[
                sm if arg.ndim == 1 else hbm if raw or i in (aliases or {}) else vm
                for i, arg in enumerate(args)
            ],
            out_specs=[at] * len(shapes),
            scratch_shapes=list(scratch),
            input_output_aliases=aliases or {},
            compiler_params=pltpu.CompilerParams(vmem_limit_bytes=limit * 1024 * 1024),
            cost_estimate=pl.CostEstimate(
                flops=flops, bytes_accessed=4 * 1024 * 1024, transcendentals=0
            ),
            name=name,
        )(*args)
    )


def attend_call(g, pos, qseg, kseg, qin, kvs, earlier=()):
    width = 2 * HEAD_DIM * (g + 1)
    scratch = [
        ((EXT, 2 * HEAD_DIM), BF),
        ((EXT, 2 * HEAD_DIM), BF),
        ((HEAD_DIM, EXT), F32),
        ((HEAD_DIM, EXT), F32),
        ((RING, ROWS, 2 * HEAD_DIM), BF),
        ((RING, ROWS, HEAD_DIM), BF),
        ((ROWS, HEAD_DIM), BF),
        ((ROWS, HEAD_DIM), BF),
        ((ROWS, 1), F32),
        ((ROWS, HEAD_DIM), F32),
        ((ROWS, WINDOW + TOK), F32),
        ((ROWS, WINDOW + TOK), BF),
        ((ROWS, WINDOW + TOK), BF),
    ]
    return call(
        functools.partial(attend, g, len(earlier)),
        "attend",
        [((TOK, 2 * HALF), BF)] * RING
        + [((ROWS, 2 * HEAD_DIM), F32)]
        + [((ROWS, width), BF)] * 2,
        (pos, qseg, kseg, *qin, *kvs, *earlier),
        [pltpu.VMEM(shape, dtype) for shape, dtype in scratch],
        flops=6 * 2 * 4 * ROWS * 1152 * 256,
        limit=40,
    )


def columns(index, width):
    return pl.ds(pl.multiple_of(index * width, width), width)


def run_copies(pairs, sem):
    copies = [pltpu.make_async_copy(src, dst, sem.at[i]) for i, (src, dst) in enumerate(pairs)]
    for copy in copies:
        copy.start()
    for copy in copies:
        copy.wait()


def pack_kv(here_ref, k_ref, v_ref, *refs):
    outs, sem = refs[:RING], refs[RING]
    pairs = []
    for d in range(RING):
        for g in range(KV):
            cols = columns(jnp.bitwise_xor(here_ref[0], d) * KV + g, HEAD_DIM)
            for ref, base in ((k_ref, 0), (v_ref, HEAD_DIM)):
                at = 2 * g * HEAD_DIM + base
                pairs.append((ref.at[:, cols], outs[d].at[:, at : at + HEAD_DIM]))
    run_copies(pairs, sem)


def pack_q(g, here_ref, q_ref, d_ref, *refs):
    outs, sem = refs[:RING], refs[RING]
    pairs = []
    for d in range(RING):
        cols = columns(jnp.bitwise_xor(here_ref[0], d) * KV + g, HALF)
        for ref, base in ((q_ref, 0), (d_ref, HALF)):
            pairs.append((ref.at[:, cols], outs[d].at[:, base : base + HALF]))
    run_copies(pairs, sem)


def add_kv(own0, own1, one, two, *outs):
    for g, own in enumerate((own0, own1)):
        cols = slice(2 * HEAD_DIM * g, 2 * HEAD_DIM * (g + 1))
        for d in range(RING):
            rows = slice(TOK * d, TOK * (d + 1))
            total = own[rows] + one[rows, cols].astype(F32) + two[rows, cols].astype(F32)
            outs[d][:, cols] = total.astype(BF)


def place_wide(g, here_ref, parts, attn, gq, sem):
    copies = []
    for d in range(RING):
        cols = columns(jnp.bitwise_xor(here_ref[0], d) * KV + g, HALF)
        for dst, base in ((attn, 0), (gq, HALF)):
            src = parts[d].at[:, base : base + HALF]
            copies.append(pltpu.make_async_copy(src, dst.at[:, cols], sem.at[len(copies)]))
    return copies


def assemble_first(here_ref, *refs):
    parts, (attn, gq, sem) = refs[:RING], refs[RING:]
    copies = place_wide(0, here_ref, parts, attn, gq, sem)
    for copy in copies:
        copy.start()
    for copy in copies:
        copy.wait()


def assemble(here_ref, *refs):
    parts, kvs = refs[2 : 2 + RING], refs[2 + RING : 2 + 2 * RING]
    attn, gq, gk, gv, sem = refs[2 + 2 * RING :]
    copies = place_wide(1, here_ref, parts, attn, gq, sem)
    for d in range(RING):
        for g in range(KV):
            cols = columns(jnp.bitwise_xor(here_ref[0], d) * KV + g, HEAD_DIM)
            for dst, base in ((gk, 2 * g * HEAD_DIM), (gv, (2 * g + 1) * HEAD_DIM)):
                src = kvs[d].at[:, base : base + HEAD_DIM]
                copies.append(pltpu.make_async_copy(src, dst.at[:, cols], sem.at[len(copies)]))
    for copy in copies:
        copy.start()
    for copy in copies:
        copy.wait()


def shards(queries, key_states, value_states, grad_output, segment_ids):
    heads = lax.axis_size("head")
    halves = lax.axis_size("blk") * heads // RING
    head = lax.axis_index("head")
    index = head % RING
    here = jnp.full((1,), index, jnp.int32)
    half = (lax.axis_index("blk") * heads + head) // RING

    def along_ring(value, d):
        return lax.ppermute(value, "head", [(i, i ^ d) for i in range(heads)])

    def along_halves(value, steps):
        count = halves * RING
        pairs = [(i, (i + steps * RING) % count) for i in range(count)]
        return lax.ppermute(value, ("blk", "head"), pairs)

    def around(parts):
        return parts[:1] + [along_ring(parts[d], d) for d in range(1, RING)]

    thin_part, wide_part = ((TOK, 2 * KV * HEAD_DIM), BF), ((TOK, 2 * HALF), BF)
    sems = [pltpu.SemaphoreType.DMA((2 * KV * RING,))]
    kv = call(
        pack_kv,
        "pack_kv",
        [thin_part] * RING,
        (here, key_states, value_states),
        sems,
        raw=True,
    )

    def pack(g, q, do):
        return call(
            functools.partial(pack_q, g),
            "pack_q",
            [wide_part] * RING,
            (here, q, do),
            sems,
            raw=True,
        )

    kv = around(kv)
    first = around(pack(0, queries, grad_output))
    kvs = []
    for g in range(KV):
        cols = slice(2 * HEAD_DIM * g, 2 * HEAD_DIM * (g + 1))
        own = jnp.concatenate([part[:, cols] for part in kv], axis=0)
        kvs.append((own, along_halves(own, 1), along_halves(own, 2)))
    late, _ = lax.optimization_barrier(((queries, grad_output), kvs[0][0]))
    q_parts = (first, around(pack(1, *late)))

    padded = jnp.concatenate([jnp.full((WINDOW,), HEAD_DIM - 1, jnp.int32), segment_ids])
    key_seg = lax.dynamic_slice_in_dim(padded, half * ROWS, EXT)
    lanes = jnp.arange(HEAD_DIM, dtype=jnp.int32)[None, :]
    kseg = (key_seg[:, None] == lanes).astype(BF)
    qseg = jnp.where(key_seg[WINDOW:, None] == lanes, 0.0, -BIG).astype(BF)
    steps = jnp.arange(RING, dtype=jnp.int32)
    pos = index ^ steps

    width = RING * KV * HALF
    wide_out, thin_out = ((TOK, width), BF), ((TOK, width // GROUP), BF)
    res0 = attend_call(0, pos, qseg, kseg, q_parts[0], kvs[0])
    wide0 = around(res0[:RING])
    res1 = attend_call(1, pos, qseg, kseg, q_parts[1], kvs[1], res0[5:])
    one, two = along_halves(res1[5], -1), along_halves(res1[6], -2)
    last, wide0 = lax.optimization_barrier((res1[:RING], wide0))
    wide1 = around(last)
    placed = call(
        assemble_first,
        "assemble_first",
        [wide_out] * 2,
        (here, *wide0),
        [pltpu.SemaphoreType.DMA((2 * RING,))],
        limit=16,
        space=pl.ANY,
    )
    grads = call(add_kv, "add_kv", [thin_part] * RING, (res0[4], res1[4], one, two), limit=16)
    grads = around(grads)
    return tuple(
        call(
            assemble,
            "assemble",
            [wide_out] * 2 + [thin_out] * 2,
            (here, *placed, *wide1, *grads),
            [pltpu.SemaphoreType.DMA((6 * RING,))],
            limit=16,
            space=pl.ANY,
            aliases={1: 0, 2: 1},
        )
    )


def solution(mesh):
    placed = P(("blk", "head"), None)
    return jax.shard_map(
        shards,
        mesh=mesh,
        in_specs=(placed, placed, placed, placed, P()),
        out_specs=(placed, placed, placed, placed),
        check_vma=False,
    )
```
